128 devices in a mesh: section: 2 (over x_hi), row: 8 (over y, core), col: 8 (over x_lo, z).
Axes of the slice: x: 4 (x_hi: 2, x_lo: 2; x = x_hi * 2 + x_lo), y: 4, z: 4, core: 2. Of those that a mesh axis runs over, the one named last changes fastest.
Arguments:
- tokens: bfloat16 [512, 12288], P(None, 'row'), may hold values from -36 to 36
- vectors: float32 [2, 12288], P('section', 'row'), may hold values from 0.5 to 1.5
- weights: bfloat16 [2, 12288, 24576], P('section', 'row', 'col'), may hold values from -0.0546875 to 0.0546875
- cotangent: bfloat16 [512, 12288], P('col', 'row'), may hold values from -6 to 6
Outputs:
- section_outputs: bfloat16 [2, 512, 12288], P('section', 'col', 'row')
- weight_grads: bfloat16 [2, 12288, 24576], P('section', 'row', 'col')
- vector_grads: float32 [2, 12288], P('section', 'row')
The draws below stay inside these ranges and needn't reach their ends.
All inputs are finite; a program needn't handle non-finite values.
Results may differ from the reference program's by a relative error of at most 0.0064.
Values may be sent and summed in bfloat16 or wider, within the bound.
No kernel may reach another device: no remote copies, remote signals or barrier semaphores. Data moves between devices by JAX's collectives and lax.ppermute only.
A program may use at most 128 MiB of HBM per device.

```python
import jax
import jax.numpy as jnp
from jax import lax

D = 12288
FFW = 24576
TOKENS = 512


def draw_tokens(key, part):
    key = jax.random.fold_in(key, 11)
    key_base, key_cols, key_rows = jax.random.split(key, 3)
    ramp = jnp.exp(jnp.log(0.5) + jnp.log(3.0) * jnp.arange(D, dtype=jnp.float32) / D)
    col_scale = ramp * jnp.exp(jax.random.uniform(key_cols, (D,), jnp.float32, jnp.log(0.5), jnp.log(2.0)))
    row_scale = jnp.exp(jax.random.uniform(key_rows, (TOKENS, 1), jnp.float32, jnp.log(0.3), jnp.log(3.0)))
    base = jnp.clip(jax.random.normal(key_base, (TOKENS, D), jnp.float32), -4.0, 4.0)
    return (base * col_scale * row_scale).astype(jnp.bfloat16)


def shard_levels(rng, shape, shards, smallest, high):
    def one(axis_at, shards_of):
        draws = jax.random.uniform(jax.random.fold_in(jax.random.fold_in(rng, 6), axis_at), (shards_of,), jnp.float32, smallest / len(shards), high / len(shards))
        return jnp.repeat(jnp.exp(draws), shape[axis_at] // shards_of).reshape((-1,) + (1,) * (len(shape) - axis_at - 1))

    loudness = one(*shards[0])
    for cut in shards[1:]:
        loudness = loudness * one(*cut)
    return loudness


def centred(own_key, extent, spread, limit, shards=(), kind=jnp.bfloat16):
    values = jax.random.normal(own_key, extent, jnp.float32) * spread
    if len(shards) > 0:
        values = shard_levels(own_key, extent, shards, -0.22, 0.18) * values
    return jnp.clip(values, min=-limit, max=limit).astype(kind)


def setup_inputs(seed: int = 0) -> dict:
    key_of = jax.random.split(jax.random.key(seed), 5)
    return {
        "tokens": draw_tokens(jax.random.fold_in(key_of[4], 71), 0),
        "vectors": jnp.clip(0.5 + 1.0 * jax.random.uniform(key_of[1], (2, D), jnp.float32) ** shard_levels(key_of[1], (2, D), ((0, 2), (1, 8)), -0.2, 0.2), 0.5, 1.5),
        "weights": centred(key_of[2], (2, D, FFW), D ** -0.5, 0.0546875, ((0, 2), (1, 8), (2, 8))),
        "cotangent": centred(key_of[3], (TOKENS, D), 1.0, 6.0, ((0, 8), (1, 8))),
    }


def activation(values):
    return jax.nn.gelu(values, approximate=True)

def reference(tokens, vectors, weights, cotangent):
    inputs = tokens.astype(jnp.float32)
    gain = vectors[0]
    bias = vectors[1]
    mean = lax.optimization_barrier(jnp.sum(inputs, axis=1)) / D
    square = lax.optimization_barrier(jnp.sum(inputs * inputs, axis=1)) / D
    inv_std = lax.rsqrt(square - mean * mean + 1e-05)
    centered = (inputs - mean[:, None]) * inv_std[:, None]
    normed = (centered * gain).astype(jnp.bfloat16)
    preact = jnp.dot(normed, weights[0], preferred_element_type=jnp.float32)
    hidden = activation(preact).astype(jnp.bfloat16)
    summed = lax.dot_general(hidden, weights[1], (((1,), (1,)), ((), ())), preferred_element_type=jnp.float32)
    output = (summed + bias).astype(jnp.bfloat16)
    bias_grad = lax.optimization_barrier(jnp.sum(cotangent.astype(jnp.float32), axis=0))
    grad_down = lax.dot_general(cotangent, hidden, (((0,), (0,)), ((), ())), preferred_element_type=jnp.float32).astype(jnp.bfloat16)
    grad_hidden = jnp.dot(cotangent, weights[1], preferred_element_type=jnp.float32).astype(jnp.bfloat16)
    _, pullback = jax.vjp(activation, preact)
    grad_pre = pullback(grad_hidden.astype(jnp.float32))[0].astype(jnp.bfloat16)
    grad_up = lax.dot_general(normed, grad_pre, (((0,), (0,)), ((), ())), preferred_element_type=jnp.float32).astype(jnp.bfloat16)
    grad_normed = lax.dot_general(grad_pre, weights[0], (((1,), (1,)), ((), ())), preferred_element_type=jnp.float32)
    gain_grad = lax.optimization_barrier(jnp.sum(grad_normed * centered, axis=0))
    grad_centered = grad_normed * gain
    mean_grad = lax.optimization_barrier(jnp.sum(grad_centered, axis=1)) / D
    slope_grad = lax.optimization_barrier(jnp.sum(grad_centered * centered, axis=1)) / D
    grad_inputs = (inv_std[:, None] * (grad_centered - mean_grad[:, None] - centered * slope_grad[:, None])).astype(jnp.bfloat16)
    return (jnp.stack([grad_inputs, output]), jnp.stack([grad_up, grad_down]), jnp.stack([gain_grad, bias_grad]))
```

```python
import jax
import jax.numpy as jnp
from jax import lax
from jax.sharding import PartitionSpec as P

D = 12288
F32 = jnp.float32
BF16 = jnp.bfloat16
CHUNKS = 1
Y_ORDERS = ((1, 3), (3, 1))
COL_ORDERS = ((1, 3, 4), (3, 4, 1), (4, 1, 3))


def exchange(block, axis, mask):
    ranks = range(lax.axis_size(axis))
    return lax.ppermute(block, axis, [(i, i ^ mask) for i in ranks])


def activation(values):
    return jax.nn.gelu(values, approximate=True)


def span(masks):
    found = [0]
    for mask in masks:
        found = found + [mask ^ f for f in found]
    return found


def scattered(block_of, send, order):
    kept = {r: block_of(r) for r in span(order)}
    for step, mask in enumerate(order):
        rest = span(order[step + 1 :])
        out = jnp.stack([kept[mask ^ q].astype(BF16) for q in rest])
        got = send(out, mask)
        kept = {q: kept[q] + got[i].astype(F32) for i, q in enumerate(rest)}
    return kept[0]


def gathered(piece, send, order):
    held = piece[None]
    relative = [0]
    for mask in order:
        held = jnp.concatenate([held, send(held, mask)])
        relative = relative + [mask ^ r for r in relative]
    return relative, held


def local(tokens, vectors, weights, cotangent):
    second = lax.axis_index("section") == 1
    row = lax.axis_index("row")
    col = lax.axis_index("col")
    core, y = row % 2, row // 2
    weight = weights[0]
    own_vector = vectors[0]
    features, hidden = weight.shape
    n = cotangent.shape[0] // CHUNKS

    def by_y(block, mask):
        return exchange(block, "row", 2 * mask)

    def by_col(block, mask):
        return exchange(block, "col", mask)

    def by_core(block):
        return exchange(block, "row", 1)

    def summed_over_y(values):
        return values + by_y(values, 1) + by_y(values, 2) + by_y(values, 3)

    def place(block):
        return ((block % 2) ^ core) * 4 + block // 2

    def own_core_first(values):
        parts = values.reshape(4, 2, CHUNKS, n, -1)
        mine = lax.dynamic_index_in_dim(parts, core, 1, keepdims=False)
        other = lax.dynamic_index_in_dim(parts, 1 - core, 1, keepdims=False)
        return jnp.stack([mine, other]).transpose(2, 0, 1, 3, 4).reshape(CHUNKS * 8 * n, -1)

    def over_row(sums):
        parts = sums.reshape(2, CHUNKS, 2, 4 * n)
        got = by_core(sums.reshape(8, 128)).reshape(2, CHUNKS, 2, 4 * n)
        return summed_over_y((parts + got[:, :, ::-1]).reshape(8, 128)).reshape(2, CHUNKS * 8 * n)

    cot_chunks = []
    for j in range(CHUNKS):
        piece = cotangent[j * n : (j + 1) * n]
        whole = jnp.zeros((8, n, features), BF16)
        width = features // 3
        for i, order in enumerate(COL_ORDERS):
            relative, held = gathered(piece[:, i * width : (i + 1) * width], by_col, order)
            for k, r in enumerate(relative):
                whole = lax.dynamic_update_slice(
                    whole, held[k : k + 1], (place(col ^ r), 0, i * width)
                )
        cot_chunks.append(whole.reshape(8 * n, features))
    cot_full = jnp.concatenate(cot_chunks)
    bias_grad = jnp.sum(cot_full.astype(F32), axis=0)

    inputs = own_core_first(tokens).astype(F32)
    sums = over_row(jnp.stack([jnp.sum(inputs, axis=1), jnp.sum(inputs * inputs, axis=1)]))
    mean, square = sums[0] / D, sums[1] / D
    inv_std = lax.rsqrt(square - mean * mean + 1e-05)
    centered = (inputs - mean[:, None]) * inv_std[:, None]
    normed = (centered * own_vector).astype(BF16)
    left = jnp.where(second, cot_full, normed)

    width = hidden // 2
    rights, products = [], []
    for j in range(CHUNKS):
        chunk = left[j * 8 * n : (j + 1) * 8 * n]
        sent = jnp.dot(chunk[4 * n :], weight, preferred_element_type=F32).astype(BF16)
        got = by_core(sent)
        kept = jnp.dot(chunk[: 4 * n], weight, preferred_element_type=F32)
        both = (kept + got.astype(F32)).reshape(4, n, hidden)
        pieces = []
        for h, order in enumerate(Y_ORDERS):
            part = both[:, :, h * width : (h + 1) * width]
            mine = scattered(
                lambda r: lax.dynamic_index_in_dim(part, y ^ r, 0, keepdims=False), by_y, order
            )
            values, pullback = jax.vjp(activation, mine)
            leaving = jnp.where(second, mine, values).astype(BF16)
            arrived = exchange(leaving, "section", 1)
            grad_pre = pullback(arrived.astype(F32))[0].astype(BF16)
            pieces.append(jnp.where(second, arrived, grad_pre))
        near = jnp.zeros((4, n, hidden), BF16)
        for h, order in enumerate(Y_ORDERS):
            relative, held = gathered(pieces[h], by_y, order)
            for k, r in enumerate(relative):
                near = lax.dynamic_update_slice(near, held[k : k + 1], (y ^ r, 0, h * width))
        near = near.reshape(4 * n, hidden)
        far = by_core(near)
        contract = (((1,), (1,)), ((), ()))
        products.append(lax.dot_general(near, weight, contract, preferred_element_type=F32))
        products.append(lax.dot_general(far, weight, contract, preferred_element_type=F32))
        rights += [near, far]

    product = jnp.concatenate(products)
    width = features // 3
    summed = []
    for j in range(CHUNKS):
        blocks = product[j * 8 * n : (j + 1) * 8 * n].reshape(8, n, features)
        thirds = []
        for i, order in enumerate(COL_ORDERS):
            part = blocks[:, :, i * width : (i + 1) * width]
            thirds.append(
                scattered(
                    lambda r: lax.dynamic_index_in_dim(part, place(col ^ r), 0, keepdims=False),
                    by_col,
                    order,
                )
            )
        summed.append(jnp.concatenate(thirds, axis=1))
    summed = jnp.concatenate(summed)

    scaled = product * own_vector
    sums = over_row(jnp.stack([jnp.sum(scaled, axis=1), jnp.sum(scaled * centered, axis=1)]))
    gain_part = jnp.sum(product * centered, axis=0)
    packed = jnp.concatenate([sums.reshape(8, 128), gain_part.reshape(-1, 128)])
    packed = packed + by_col(packed, 1) + by_col(packed, 2) + by_col(packed, 3)
    packed = packed + by_col(packed, 4)
    sums, gain_grad = packed[:8].reshape(2, -1), packed[8:].reshape(-1)

    right = jnp.concatenate(rights)
    weight_grads = lax.dot_general(
        left, right, (((0,), (0,)), ((), ())), preferred_element_type=F32
    ).astype(BF16)

    def own_tokens(values):
        parts = values.reshape((CHUNKS, 8, n) + values.shape[1:])
        found = lax.dynamic_index_in_dim(parts, place(col), 1, keepdims=False)
        return found.reshape((CHUNKS * n,) + values.shape[1:])

    mean_grad, slope_grad = own_tokens(sums[0]) / D, own_tokens(sums[1]) / D
    grad_inputs = own_tokens(inv_std)[:, None] * (
        summed * own_vector - mean_grad[:, None] - own_tokens(centered) * slope_grad[:, None]
    )
    output = summed + own_vector
    section_outputs = jnp.where(second, output, grad_inputs).astype(BF16)[None]
    vector_grads = jnp.where(second, bias_grad, gain_grad)[None]
    return (section_outputs, weight_grads[None], vector_grads)


def solution(mesh):
    in_specs = (P(None, "row"), P("section", "row"), P("section", "row", "col"), P("col", "row"))
    out_specs = (P("section", "col", "row"), P("section", "row", "col"), P("section", "row"))
    return jax.shard_map(local, mesh=mesh, in_specs=in_specs, out_specs=out_specs, check_vma=False)
```

```python
import jax
import jax.numpy as jnp
from jax import lax
from jax.sharding import PartitionSpec as P

D = 12288
F32 = jnp.float32
BF16 = jnp.bfloat16
Y_ORDERS = ((1, 3), (3, 1))
Y_PLACES = (0, 1, 3, 2)
COL_ORDERS = ((1, 3, 4), (3, 4, 1), (4, 1, 3))
CONTRACT_LAST = (((1,), (1,)), ((), ()))
CONTRACT_FIRST = (((0,), (0,)), ((), ()))


def exchange(block, axis, mask):
    ranks = range(lax.axis_size(axis))
    return lax.ppermute(block, axis, [(i, i ^ mask) for i in ranks])


def transposed(block):
    rows, cols = lax.axis_size("row"), lax.axis_size("col")
    route = [(r * cols + c, c * cols + r) for r in range(rows) for c in range(cols)]
    return lax.ppermute(block, ("section", "row", "col"), route)


def activation(values):
    return jax.nn.gelu(values, approximate=True)


def span(masks):
    found = [0]
    for mask in masks:
        found = found + [mask ^ f for f in found]
    return found


def local(tokens, vectors, weights, cotangent):
    second = lax.axis_index("section") == 1
    row = lax.axis_index("row")
    col = lax.axis_index("col")
    weight = weights[0]
    own_vector = vectors[0]
    features, hidden = weight.shape
    n = cotangent.shape[0]

    def by_y(block, mask):
        return exchange(block, "row", 2 * mask)

    def place(block):
        relative = block ^ row
        y = relative // 2
        return (relative % 2) * 4 + (y ^ (y // 2))

    width = features // 3
    held = [cotangent[None, :, i * width : (i + 1) * width] for i in range(3)]
    relative = [[0], [0], [0]]
    inputs = tokens.astype(F32)
    sums = None
    for step in range(3):
        got = [exchange(held[i], "col", order[step]) for i, order in enumerate(COL_ORDERS)]
        if step == 0:
            inputs, held = lax.optimization_barrier((inputs, held))
            sums = jnp.concatenate([jnp.sum(inputs, axis=1), jnp.sum(inputs * inputs, axis=1)])
        sums = sums + exchange(sums, "row", (1, 2, 4)[step])
        held = [jnp.concatenate([h, g]) for h, g in zip(held, got)]
        relative = [
            rel + [order[step] ^ r for r in rel] for rel, order in zip(relative, COL_ORDERS)
        ]
        if step < 2:
            held, sums = lax.optimization_barrier((held, sums))
    whole = jnp.zeros((8, n, features), BF16)
    for i in range(3):
        for k, r in enumerate(relative[i]):
            whole = lax.dynamic_update_slice(
                whole, held[i][k : k + 1], (place(col ^ r), 0, i * width)
            )
    cot_full = whole.reshape(8 * n, features)
    bias_grad = jnp.sum(cot_full.astype(F32), axis=0)
    total_rows = tokens.shape[0]
    mean, square = sums[:total_rows] / D, sums[total_rows:] / D
    inv_std = lax.rsqrt(square - mean * mean + 1e-05)
    normed = ((inputs - mean[:, None]) * inv_std[:, None] * own_vector).astype(BF16)
    blocks = [row ^ (2 * y + core) for core in range(2) for y in Y_PLACES]
    normed = jnp.concatenate([lax.dynamic_slice_in_dim(normed, b * n, n, 0) for b in blocks])
    left = jnp.where(second, cot_full, normed)

    sent = jnp.dot(left[4 * n :], weight, preferred_element_type=F32).astype(BF16)
    got = exchange(sent, "row", 1)
    kept = jnp.dot(left[: 4 * n], weight, preferred_element_type=F32)
    kept = lax.optimization_barrier(kept)
    both = (kept + got.astype(F32)).reshape(4, n, hidden)
    high = own_vector.astype(BF16)
    low = (own_vector - high.astype(F32)).astype(BF16)
    gain_rows = jnp.stack([high, low] + [jnp.zeros_like(high)] * 6)
    gain_image = None
    width = hidden // 2
    parts = [
        {r: both[i, :, h * width : (h + 1) * width] for i, r in enumerate(Y_PLACES)}
        for h in range(2)
    ]
    for step in range(2):
        sends = []
        for part, order in zip(parts, Y_ORDERS):
            rest = span(order[step + 1 :])
            sends.append(jnp.stack([part[order[step] ^ q].astype(BF16) for q in rest]))
        sends, gain_rows, gain_image = lax.optimization_barrier((sends, gain_rows, gain_image))
        got = [by_y(s, order[step]) for s, order in zip(sends, Y_ORDERS)]
        if step == 0:
            gain_image = jnp.dot(gain_rows, weight, preferred_element_type=F32)
            gain_image = jnp.sum(gain_image, axis=0)
        gain_image = gain_image + exchange(gain_image, "row", (1, 2)[step])
        parts = [
            {q: part[q] + g[i].astype(F32) for i, q in enumerate(span(order[step + 1 :]))}
            for part, g, order in zip(parts, got, Y_ORDERS)
        ]
    mine = jnp.concatenate([parts[0][0], parts[1][0]], axis=1)

    values, pullback = jax.vjp(activation, mine)
    leaving = jnp.where(second, mine, values).astype(BF16)
    leaving, gain_image = lax.optimization_barrier((leaving, gain_image))
    arrived = exchange(leaving, "section", 1)
    gain_image = gain_image + exchange(gain_image, "row", 4)
    grad_pre = pullback(arrived.astype(F32))[0].astype(BF16)
    piece = jnp.where(second, arrived, grad_pre)
    grads = piece.astype(F32)
    token_sums = jnp.concatenate([jnp.sum(grads * gain_image, axis=1), jnp.sum(grads * mine, axis=1)])
    held = [piece[None, :, :width], piece[None, :, width:]]
    got = [by_y(h, order[0]) for h, order in zip(held, Y_ORDERS)]
    token_sums = token_sums + exchange(token_sums, "col", 1)
    held = [jnp.concatenate([h, g]) for h, g in zip(held, got)]
    held, token_sums = lax.optimization_barrier((held, token_sums))
    got = [by_y(h, order[1]) for h, order in zip(held, Y_ORDERS)]
    token_sums = token_sums + exchange(token_sums, "col", 2)
    near = jnp.concatenate(
        [
            jnp.concatenate([held[0], got[0]]).reshape(4 * n, width),
            jnp.stack([held[1], got[1]], axis=1).reshape(4 * n, width),
        ],
        axis=1,
    )
    near, token_sums = lax.optimization_barrier((near, token_sums))
    far = exchange(near, "row", 1)
    token_sums = token_sums + exchange(token_sums, "col", 4)

    product = jnp.concatenate(
        [
            lax.dot_general(near, weight, CONTRACT_LAST, preferred_element_type=F32),
            lax.dot_general(far, weight, CONTRACT_LAST, preferred_element_type=F32),
        ]
    )
    gain_grad = jnp.sum(product * left.astype(F32), axis=0) / own_vector
    width = features // 3
    split = product.reshape(8, n, features)
    parts = [
        {
            r: lax.dynamic_slice(split, (place(col ^ r), 0, i * width), (1, n, width))
            for r in range(8)
        }
        for i in range(3)
    ]
    right = jnp.concatenate([near, far])
    weight_grads = None
    for step in range(3):
        sends = []
        for part, order in zip(parts, COL_ORDERS):
            rest = span(order[step + 1 :])
            sends.append(jnp.concatenate([part[order[step] ^ q].astype(BF16) for q in rest]))
        sends, right, gain_grad, token_sums = lax.optimization_barrier(
            (sends, right, gain_grad, token_sums)
        )
        got = [exchange(s, "col", order[step]) for s, order in zip(sends, COL_ORDERS)]
        gain_grad = gain_grad + exchange(gain_grad, "col", (1, 2, 4)[step])
        if step == 0:
            weight_grads = lax.dot_general(
                left, right, CONTRACT_FIRST, preferred_element_type=F32
            ).astype(BF16)
            weight_grads, got = lax.optimization_barrier((weight_grads, got))
        parts = [
            {q: part[q] + g[i : i + 1].astype(F32) for i, q in enumerate(span(order[step + 1 :]))}
            for part, g, order in zip(parts, got, COL_ORDERS)
        ]
    token_sums = transposed(token_sums) / D
    mean_grad, slope_grad = token_sums[:n], token_sums[n:]
    summed = jnp.concatenate([part[0][0] for part in parts], axis=1)

    first_row = col * n
    own_mean = lax.dynamic_slice_in_dim(mean, first_row, n, 0)
    own_inv = lax.dynamic_slice_in_dim(inv_std, first_row, n, 0)
    own_inputs = lax.dynamic_slice_in_dim(tokens, first_row, n, 0).astype(F32)
    own_centered = (own_inputs - own_mean[:, None]) * own_inv[:, None]
    grad_inputs = own_inv[:, None] * (
        summed * own_vector - mean_grad[:, None] - own_centered * slope_grad[:, None]
    )
    output = summed + own_vector
    section_outputs = jnp.where(second, output, grad_inputs).astype(BF16)[None]
    vector_grads = jnp.where(second, bias_grad, gain_grad)[None]
    return (section_outputs, weight_grads[None], vector_grads)


def solution(mesh):
    in_specs = (P(None, "row"), P("section", "row"), P("section", "row", "col"), P("col", "row"))
    out_specs = (P("section", "col", "row"), P("section", "row", "col"), P("section", "row"))
    return jax.shard_map(local, mesh=mesh, in_specs=in_specs, out_specs=out_specs, check_vma=False)
```

```python
import jax
import jax.numpy as jnp
from jax import lax
from jax.sharding import PartitionSpec as P

D = 12288
F32 = jnp.float32
BF16 = jnp.bfloat16
CHUNKS = 2
COL_ORDERS = ((1, 3, 4), (3, 4, 1), (4, 1, 3))
CONTRACT_LAST = (((1,), (1,)), ((), ()))
CONTRACT_FIRST = (((0,), (0,)), ((), ()))


def exchange(block, axis, mask):
    ranks = range(lax.axis_size(axis))
    return lax.ppermute(block, axis, [(i, i ^ mask) for i in ranks])


def mask_of(core, turn):
    return 1 + 2 * (core ^ turn)


def over_y(block, turn):
    ranks = range(lax.axis_size("row"))
    return lax.ppermute(block, "row", [(i, i ^ (2 * mask_of(i % 2, turn))) for i in ranks])


def over_z(block, turn):
    rows, cols = lax.axis_size("row"), lax.axis_size("col")
    route = [
        (r * cols + c, r * cols + (c ^ mask_of(r % 2, turn)))
        for r in range(rows)
        for c in range(cols)
    ]
    return lax.ppermute(block, ("row", "col"), route)


def activation(values):
    return jax.nn.gelu(values, approximate=True)


def local(tokens, vectors, weights, cotangent):
    second = lax.axis_index("section") == 1
    row = lax.axis_index("row")
    col = lax.axis_index("col")
    core = row % 2
    weight = weights[0]
    own_vector = vectors[0]
    features, hidden = weight.shape
    block_rows = cotangent.shape[0]
    n = block_rows // CHUNKS
    total_rows = tokens.shape[0]
    chunks = range(CHUNKS)
    first, then = mask_of(core, 0), mask_of(core, 1)
    col_order = [6, 2, first ^ 4, first, then ^ 4, then, 4, 0]

    def block_at(place):
        other, q = place // 4, place % 4
        y = (2, mask_of(core ^ other, 0), mask_of(core ^ other, 1), 0)[q]
        return row ^ (2 * y + other)

    def place_of(block):
        relative = block ^ row
        y, other = relative // 2, relative % 2
        odd = 1 + ((y // 2) ^ core ^ other)
        return other * 4 + jnp.where(y % 2 == 1, odd, jnp.where(y == 2, 0, 3))

    width = features // 3
    held = [cotangent[None, :, i * width : (i + 1) * width] for i in range(3)]
    relative = [[0], [0], [0]]
    for step in range(3):
        got = [exchange(held[i], "col", order[step]) for i, order in enumerate(COL_ORDERS)]
        if step == 1:
            inputs = tokens.astype(F32)
            sums = jnp.concatenate([jnp.sum(inputs, axis=1), jnp.sum(inputs * inputs, axis=1)])
            sums = sums + exchange(sums, "row", 1)
            image_start = jnp.sum(weight[:8].astype(F32) * own_vector[:8, None], axis=0)
        held = [jnp.concatenate([h, g]) for h, g in zip(held, got)]
        relative = [
            rel + [order[step] ^ r for r in rel] for rel, order in zip(relative, COL_ORDERS)
        ]
        if step == 0:
            held, tokens, own_vector = lax.optimization_barrier((held, tokens, own_vector))
        if step == 1:
            held, sums, image_start = lax.optimization_barrier((held, sums, image_start))
    sums = sums + exchange(sums, "row", 2)
    sums = sums + exchange(sums, "row", 4)
    whole = jnp.zeros((8, block_rows, features), BF16)
    for i in range(3):
        for k, r in enumerate(relative[i]):
            whole = lax.dynamic_update_slice(
                whole, held[i][k : k + 1], (place_of(col ^ r), 0, i * width)
            )
    mean, square = sums[:total_rows] / D, sums[total_rows:] / D
    inv_std = lax.rsqrt(square - mean * mean + 1e-05)
    normed_rows = ((inputs - mean[:, None]) * inv_std[:, None] * own_vector).astype(BF16)
    cots, norms = [], []
    for c in chunks:
        cots.append(whole[:, c * n : (c + 1) * n].reshape(8 * n, features))
        norms.append(
            jnp.concatenate(
                [
                    lax.dynamic_slice_in_dim(normed_rows, block_at(k) * block_rows + c * n, n, 0)
                    for k in range(8)
                ]
            )
        )

    both, sent = [], []
    for c in chunks:
        left = jnp.where(second, cots[c], norms[c])
        partial = jnp.dot(left, weight, preferred_element_type=F32)
        partial = lax.optimization_barrier(partial)
        both.append(partial[: 4 * n])
        sent.append(exchange(partial[4 * n :].astype(BF16), "row", 1))
    both = [(b + g.astype(F32)).reshape(4, n, hidden) for b, g in zip(both, sent)]
    send = [b[:2].astype(BF16) for b in both]
    later = jnp.where(lax.iota(jnp.int32, features) < 8, 0.0, own_vector)
    high = later.astype(BF16)
    low = (later - high.astype(F32)).astype(BF16)
    gain_rows = jnp.stack([high, low] + [jnp.zeros_like(high)] * 6)
    send[-1], gain_rows, cots, norms = lax.optimization_barrier((send[-1], gain_rows, cots, norms))
    got = [over_y(s, 0) for s in send]
    gain_image = jnp.dot(gain_rows, weight, preferred_element_type=F32)
    gain_image = jnp.sum(gain_image, axis=0) + image_start
    gain_image = gain_image + exchange(gain_image, "row", 1)
    left = jnp.concatenate([jnp.where(second, cots[c], norms[c]) for c in chunks])
    both = [b[2:] + g.astype(F32) for b, g in zip(both, got)]
    send = [b[:1].astype(BF16) for b in both]
    send[-1], gain_image = lax.optimization_barrier((send[-1], gain_image))
    got = [over_y(s, 1) for s in send]
    gain_image = gain_image + exchange(gain_image, "row", 2)
    mine = [b[1] + g[0].astype(F32) for b, g in zip(both, got)]

    leaving, pullbacks = [], []
    for c in chunks:
        values, pullback = jax.vjp(activation, mine[c])
        leaving.append(jnp.where(second, mine[c], values).astype(BF16))
        pullbacks.append(pullback)
    leaving[-1], gain_image, mean, inv_std = lax.optimization_barrier(
        (leaving[-1], gain_image, mean, inv_std)
    )
    arrived = [exchange(l, "section", 1) for l in leaving]
    gain_image = gain_image + exchange(gain_image, "row", 4)
    first_row = col * block_rows
    own_mean = lax.dynamic_slice_in_dim(mean, first_row, block_rows, 0)
    own_inv = lax.dynamic_slice_in_dim(inv_std, first_row, block_rows, 0)
    own_inputs = lax.dynamic_slice_in_dim(tokens, first_row, block_rows, 0).astype(F32)
    own_centered = (own_inputs - own_mean[:, None]) * own_inv[:, None]
    pieces = [
        jnp.where(second, a, pullbacks[c](a.astype(F32))[0].astype(BF16))
        for c, a in enumerate(arrived)
    ]
    held = []
    for p, m in zip(pieces, mine):
        grads = p.astype(F32)
        token_sums = [
            jnp.sum(grads * gain_image, axis=1, keepdims=True),
            jnp.sum(grads * m, axis=1, keepdims=True),
        ]
        token_sums = [t.astype(BF16) for t in token_sums]
        held.append(jnp.concatenate([p] + token_sums + [jnp.zeros((n, 126), BF16)], axis=1)[None])
    got = [over_y(h, 1) for h in held]
    held = [jnp.concatenate([g, h]) for g, h in zip(got, held)]
    held[-1], own_centered, own_inv = lax.optimization_barrier((held[-1], own_centered, own_inv))
    got = [over_y(h, 0) for h in held]
    near = [jnp.concatenate([g, h]).reshape(4 * n, -1) for g, h in zip(got, held)]
    far = [exchange(x, "row", 1) for x in near]

    rights = [jnp.concatenate([x[:, :hidden], f[:, :hidden]]) for x, f in zip(near, far)]
    extras = [jnp.concatenate([x[:, hidden:], f[:, hidden:]]) for x, f in zip(near, far)]
    products = [
        lax.dot_general(r, weight, CONTRACT_LAST, preferred_element_type=F32) for r in rights
    ]
    parts = []
    for p, e in zip(products, extras):
        split = p.reshape(8, n, features)
        beside = e.astype(F32).reshape(8, n, 128)
        blocks = []
        for r in col_order:
            place = place_of(col ^ r)
            blocks.append(
                jnp.concatenate(
                    [
                        lax.dynamic_slice_in_dim(split, place, 1, 0),
                        lax.dynamic_slice_in_dim(beside, place, 1, 0),
                    ],
                    axis=2,
                )
            )
        parts.append(jnp.concatenate(blocks))
    send = [p[:4].astype(BF16) for p in parts]
    products, left = lax.optimization_barrier((products, left))
    gain_grad = jnp.sum(jnp.concatenate(products) * left.astype(F32), axis=0) / own_vector
    bias_grad = jnp.sum(left.astype(F32), axis=0)
    right = jnp.concatenate(rights)
    send[-1], right, gain_grad = lax.optimization_barrier((send[-1], right, gain_grad))
    got = [over_z(s, 0) for s in send]
    gain_grad = gain_grad + exchange(gain_grad, "col", 1)
    right, gain_grad = lax.optimization_barrier((right, gain_grad))
    gain_grad = gain_grad + exchange(gain_grad, "col", 2)
    weight_grads = lax.dot_general(
        left, right, CONTRACT_FIRST, preferred_element_type=F32
    ).astype(BF16)
    weight_grads, got = lax.optimization_barrier((weight_grads, got))
    parts = [p[4:] + g.astype(F32) for p, g in zip(parts, got)]
    send = [p[:2].astype(BF16) for p in parts]
    send[-1], gain_grad = lax.optimization_barrier((send[-1], gain_grad))
    got = [over_z(s, 1) for s in send]
    other_gain = exchange(gain_grad, "col", 4)
    got, other_gain = lax.optimization_barrier((got, other_gain))
    gain_grad = gain_grad + other_gain
    parts = [p[2:] + g.astype(F32) for p, g in zip(parts, got)]
    summed = jnp.concatenate(
        [p[1] + exchange(p[0].astype(BF16), "col", 4).astype(F32) for p in parts]
    )

    mean_grad = summed[:, features : features + 1] / D
    slope_grad = summed[:, features + 1 : features + 2] / D
    summed = summed[:, :features]
    grad_inputs = own_inv[:, None] * (
        summed * own_vector - mean_grad - own_centered * slope_grad
    )
    output = summed + own_vector
    section_outputs = jnp.where(second, output, grad_inputs).astype(BF16)[None]
    vector_grads = jnp.where(second, bias_grad, gain_grad)[None]
    return (section_outputs, weight_grads[None], vector_grads)


def solution(mesh):
    in_specs = (P(None, "row"), P("section", "row"), P("section", "row", "col"), P("col", "row"))
    out_specs = (P("section", "col", "row"), P("section", "row", "col"), P("section", "row"))
    return jax.shard_map(local, mesh=mesh, in_specs=in_specs, out_specs=out_specs, check_vma=False)
```

```python
import jax
import jax.numpy as jnp
from jax import lax
from jax.sharding import PartitionSpec as P

D = 12288
F32 = jnp.float32
BF16 = jnp.bfloat16
CHUNKS = 2
COL_ORDERS = ((1, 3, 4), (3, 4, 1), (4, 1, 3))
CONTRACT_LAST = (((1,), (1,)), ((), ()))
CONTRACT_FIRST = (((0,), (0,)), ((), ()))


def exchange(block, axis, mask):
    ranks = range(lax.axis_size(axis))
    return lax.ppermute(block, axis, [(i, i ^ mask) for i in ranks])


def mask_of(core, turn):
    return 1 + 2 * (core ^ turn)


def over_y(block, turn):
    ranks = range(lax.axis_size("row"))
    return lax.ppermute(block, "row", [(i, i ^ (2 * mask_of(i % 2, turn))) for i in ranks])


def over_z(block, turn):
    rows, cols = lax.axis_size("row"), lax.axis_size("col")
    route = [
        (r * cols + c, r * cols + (c ^ mask_of(r % 2, turn)))
        for r in range(rows)
        for c in range(cols)
    ]
    return lax.ppermute(block, ("row", "col"), route)


def activation(values):
    return jax.nn.gelu(values, approximate=True)


def local(tokens, vectors, weights, cotangent):
    second = lax.axis_index("section") == 1
    row = lax.axis_index("row")
    col = lax.axis_index("col")
    core = row % 2
    weight = weights[0]
    own_vector = vectors[0]
    features, hidden = weight.shape
    block_rows = cotangent.shape[0]
    n = block_rows // CHUNKS
    total_rows = tokens.shape[0]
    chunks = range(CHUNKS)
    first, then = mask_of(core, 0), mask_of(core, 1)
    col_order = [6, 2, first ^ 4, first, then ^ 4, then, 4, 0]

    def block_at(place):
        other, q = place // 4, place % 4
        y = (2, mask_of(core ^ other, 0), mask_of(core ^ other, 1), 0)[q]
        return row ^ (2 * y + other)

    def place_of(block):
        relative = block ^ row
        y, other = relative // 2, relative % 2
        odd = 1 + ((y // 2) ^ core ^ other)
        return other * 4 + jnp.where(y % 2 == 1, odd, jnp.where(y == 2, 0, 3))

    width = features // 3
    held = [cotangent[None, :, i * width : (i + 1) * width] for i in range(3)]
    relative = [[0], [0], [0]]
    for step in range(3):
        got = [exchange(held[i], "col", order[step]) for i, order in enumerate(COL_ORDERS)]
        if step == 1:
            inputs = tokens.astype(F32)
            sums = jnp.concatenate([jnp.sum(inputs, axis=1), jnp.sum(inputs * inputs, axis=1)])
            sums = sums + exchange(sums, "row", 1)
            image_start = jnp.sum(
                weight[:8].astype(F32) * own_vector[:8, None], axis=0, keepdims=True
            )
        held = [jnp.concatenate([h, g]) for h, g in zip(held, got)]
        relative = [
            rel + [order[step] ^ r for r in rel] for rel, order in zip(relative, COL_ORDERS)
        ]
        if step == 0:
            held, tokens, own_vector = lax.optimization_barrier((held, tokens, own_vector))
        if step == 1:
            held, sums, image_start = lax.optimization_barrier((held, sums, image_start))
    sums = sums + exchange(sums, "row", 2)
    sums = sums + exchange(sums, "row", 4)
    whole = jnp.zeros((8, block_rows, features), BF16)
    for i in range(3):
        for k, r in enumerate(relative[i]):
            whole = lax.dynamic_update_slice(
                whole, held[i][k : k + 1], (place_of(col ^ r), 0, i * width)
            )
    mean, square = sums[:total_rows] / D, sums[total_rows:] / D
    inv_std = lax.rsqrt(square - mean * mean + 1e-05)
    normed_rows = ((inputs - mean[:, None]) * inv_std[:, None] * own_vector).astype(BF16)
    cots, norms = [], []
    for c in chunks:
        cots.append(whole[:, c * n : (c + 1) * n].reshape(8 * n, features))
        norms.append(
            jnp.concatenate(
                [
                    lax.dynamic_slice_in_dim(normed_rows, block_at(k) * block_rows + c * n, n, 0)
                    for k in range(8)
                ]
            )
        )

    both, sent = [], []
    for c in chunks:
        left = jnp.where(second, cots[c], norms[c])
        partial = jnp.dot(left, weight, preferred_element_type=F32)
        partial = lax.optimization_barrier(partial)
        both.append(partial[: 4 * n])
        sent.append(exchange(partial[4 * n :].astype(BF16), "row", 1))
    both = [(b + g.astype(F32)).reshape(4, n, hidden) for b, g in zip(both, sent)]
    send = [b[:2].astype(BF16) for b in both]
    later = jnp.where(lax.iota(jnp.int32, features) < 8, 0.0, own_vector)
    high = later.astype(BF16)
    low = (later - high.astype(F32)).astype(BF16)
    gain_rows = jnp.stack([high, low] + [jnp.zeros_like(high)] * 6)
    send[-1], gain_rows, cots, norms = lax.optimization_barrier((send[-1], gain_rows, cots, norms))
    got = [over_y(s, 0) for s in send]
    gain_image = jnp.dot(gain_rows, weight, preferred_element_type=F32)
    gain_image = jnp.sum(gain_image, axis=0, keepdims=True) + image_start
    gain_image = gain_image + exchange(gain_image, "row", 1)
    left = jnp.concatenate([jnp.where(second, cots[c], norms[c]) for c in chunks])
    both = [b[2:] + g.astype(F32) for b, g in zip(both, got)]
    send = [b[:1].astype(BF16) for b in both]
    send[-1], gain_image = lax.optimization_barrier((send[-1], gain_image))
    got = [over_y(s, 1) for s in send]
    gain_image = gain_image + exchange(gain_image, "row", 2)
    mine = [b[1] + g[0].astype(F32) for b, g in zip(both, got)]

    leaving, pullbacks = [], []
    for c in chunks:
        values, pullback = jax.vjp(activation, mine[c])
        leaving.append(jnp.where(second, mine[c], values).astype(BF16))
        pullbacks.append(pullback)
    leaving[-1], gain_image, mean, inv_std = lax.optimization_barrier(
        (leaving[-1], gain_image, mean, inv_std)
    )
    arrived = [exchange(l, "section", 1) for l in leaving]
    gain_image = gain_image + exchange(gain_image, "row", 4)
    first_row = col * block_rows
    own_mean = lax.dynamic_slice_in_dim(mean, first_row, block_rows, 0)
    own_inv = lax.dynamic_slice_in_dim(inv_std, first_row, block_rows, 0)
    own_inputs = lax.dynamic_slice_in_dim(tokens, first_row, block_rows, 0).astype(F32)
    own_centered = (own_inputs - own_mean[:, None]) * own_inv[:, None]
    held = []
    columns = lax.broadcasted_iota(jnp.int32, (n, hidden + 128), 1)
    for c in chunks:
        a, m = arrived[c], mine[c]
        p = jnp.where(second, a, pullbacks[c](a.astype(F32))[0].astype(BF16))
        p, m = lax.optimization_barrier((p, m))
        grads = p.astype(F32)
        a_sum = jnp.sum(grads * gain_image, axis=1, keepdims=True)
        b_sum = jnp.sum(grads * m, axis=1, keepdims=True)
        wide = jnp.pad(p, ((0, 0), (0, 128))).astype(F32)
        wide = jnp.where(columns == hidden, a_sum, wide)
        wide = jnp.where(columns == hidden + 1, b_sum, wide)
        held.append(wide.astype(BF16)[None])
        if c + 1 < CHUNKS:
            arrived[c + 1], _ = lax.optimization_barrier((arrived[c + 1], held[c]))
    got = [over_y(h, 1) for h in held]
    held = [jnp.concatenate([g, h]) for g, h in zip(got, held)]
    held[-1], own_centered, own_inv = lax.optimization_barrier((held[-1], own_centered, own_inv))
    got = [over_y(h, 0) for h in held]
    near = [jnp.concatenate([g, h]).reshape(4 * n, -1) for g, h in zip(got, held)]
    far = [exchange(x, "row", 1) for x in near]

    rights = [jnp.concatenate([x[:, :hidden], f[:, :hidden]]) for x, f in zip(near, far)]
    extras = [jnp.concatenate([x[:, hidden:], f[:, hidden:]]) for x, f in zip(near, far)]
    products = [
        lax.dot_general(r, weight, CONTRACT_LAST, preferred_element_type=F32) for r in rights
    ]
    parts = []
    for p, e in zip(products, extras):
        split = p.reshape(8, n, features)
        beside = e.astype(F32).reshape(8, n, 128)
        blocks = []
        for r in col_order:
            place = place_of(col ^ r)
            blocks.append(
                jnp.concatenate(
                    [
                        lax.dynamic_slice_in_dim(split, place, 1, 0),
                        lax.dynamic_slice_in_dim(beside, place, 1, 0),
                    ],
                    axis=2,
                )
            )
        parts.append(jnp.concatenate(blocks))
    send = [p[:4].astype(BF16) for p in parts]
    products, left = lax.optimization_barrier((products, left))
    gain_grad = jnp.sum(jnp.concatenate(products) * left.astype(F32), axis=0) / own_vector
    bias_grad = jnp.sum(left.astype(F32), axis=0)
    right = jnp.concatenate(rights)
    send[-1], right, gain_grad = lax.optimization_barrier((send[-1], right, gain_grad))
    got = [over_z(s, 0) for s in send]
    gain_grad = gain_grad + exchange(gain_grad, "col", 1)
    right, gain_grad = lax.optimization_barrier((right, gain_grad))
    gain_grad = gain_grad + exchange(gain_grad, "col", 2)
    weight_grads = lax.dot_general(
        left, right, CONTRACT_FIRST, preferred_element_type=F32
    ).astype(BF16)
    weight_grads, got = lax.optimization_barrier((weight_grads, got))
    parts = [p[4:] + g.astype(F32) for p, g in zip(parts, got)]
    send = [p[:2].astype(BF16) for p in parts]
    send[-1], gain_grad = lax.optimization_barrier((send[-1], gain_grad))
    got = [over_z(x, 1) for x in send]
    other_gain = exchange(gain_grad, "col", 4)
    parts = [p[2:] + g.astype(F32) for p, g in zip(parts, got)]
    got = [exchange(p[0].astype(BF16), "col", 4) for p in parts]
    got[-1], other_gain = lax.optimization_barrier((got[-1], other_gain))
    gain_grad = gain_grad + other_gain
    summed = jnp.concatenate([p[1] + g.astype(F32) for p, g in zip(parts, got)])
    mean_grad = summed[:, features : features + 1] / D
    slope_grad = summed[:, features + 1 : features + 2] / D
    summed = summed[:, :features]
    grad_inputs = own_inv[:, None] * (
        summed * own_vector - mean_grad - own_centered * slope_grad
    )
    output = summed + own_vector
    section_outputs = jnp.where(second, output, grad_inputs).astype(BF16)[None]
    vector_grads = jnp.where(second, bias_grad, gain_grad)[None]
    return (section_outputs, weight_grads[None], vector_grads)


def solution(mesh):
    in_specs = (P(None, "row"), P("section", "row"), P("section", "row", "col"), P("col", "row"))
    out_specs = (P("section", "col", "row"), P("section", "row", "col"), P("section", "row"))
    return jax.shard_map(local, mesh=mesh, in_specs=in_specs, out_specs=out_specs, check_vma=False)
```

```python
import jax
import jax.numpy as jnp
from jax import lax
from jax.sharding import PartitionSpec as P

D = 12288
F32 = jnp.float32
BF16 = jnp.bfloat16
CHUNKS = 2
COL_ORDERS = ((1, 3, 4), (3, 4, 1), (4, 1, 3))
CONTRACT_LAST = (((1,), (1,)), ((), ()))
CONTRACT_FIRST = (((0,), (0,)), ((), ()))


def exchange(block, axis, mask):
    ranks = range(lax.axis_size(axis))
    return lax.ppermute(block, axis, [(i, i ^ mask) for i in ranks])


def mask_of(core, turn):
    return 1 + 2 * (core ^ turn)


def over_y(block, turn):
    ranks = range(lax.axis_size("row"))
    return lax.ppermute(block, "row", [(i, i ^ (2 * mask_of(i % 2, turn))) for i in ranks])


def over_z(block, turn):
    rows, cols = lax.axis_size("row"), lax.axis_size("col")
    route = [
        (r * cols + c, r * cols + (c ^ mask_of(r % 2, turn)))
        for r in range(rows)
        for c in range(cols)
    ]
    return lax.ppermute(block, ("row", "col"), route)


def activation(values):
    return jax.nn.gelu(values, approximate=True)


def local(tokens, vectors, weights, cotangent):
    second = lax.axis_index("section") == 1
    row = lax.axis_index("row")
    col = lax.axis_index("col")
    core = row % 2
    weight = weights[0]
    own_vector = vectors[0]
    features, hidden = weight.shape
    block_rows = cotangent.shape[0]
    n = block_rows // CHUNKS
    total_rows = tokens.shape[0]
    chunks = range(CHUNKS)
    first, then = mask_of(core, 0), mask_of(core, 1)
    col_order = [6, 2, first ^ 4, first, then ^ 4, then, 4, 0]

    def block_at(place):
        other, q = place // 4, place % 4
        y = (2, mask_of(core ^ other, 0), mask_of(core ^ other, 1), 0)[q]
        return row ^ (2 * y + other)

    def place_of(block):
        relative = block ^ row
        y, other = relative // 2, relative % 2
        odd = 1 + ((y // 2) ^ core ^ other)
        return other * 4 + jnp.where(y % 2 == 1, odd, jnp.where(y == 2, 0, 3))

    width = features // 3
    held = [cotangent[None, :, i * width : (i + 1) * width] for i in range(3)]
    relative = [[0], [0], [0]]
    for step in range(3):
        got = [exchange(held[i], "col", order[step]) for i, order in enumerate(COL_ORDERS)]
        if step == 1:
            inputs = tokens.astype(F32)
            sums = jnp.concatenate([jnp.sum(inputs, axis=1), jnp.sum(inputs * inputs, axis=1)])
            sums = sums + exchange(sums, "row", 1)
            image_start = jnp.sum(
                weight[:8].astype(F32) * own_vector[:8, None], axis=0, keepdims=True
            )
        held = [jnp.concatenate([h, g]) for h, g in zip(held, got)]
        relative = [
            rel + [order[step] ^ r for r in rel] for rel, order in zip(relative, COL_ORDERS)
        ]
        if step == 0:
            held, tokens, own_vector = lax.optimization_barrier((held, tokens, own_vector))
        if step == 1:
            held, sums, image_start = lax.optimization_barrier((held, sums, image_start))
    sums = sums + exchange(sums, "row", 2)
    sums = sums + exchange(sums, "row", 4)
    whole = jnp.zeros((8, block_rows, features), BF16)
    for i in range(3):
        for k, r in enumerate(relative[i]):
            whole = lax.dynamic_update_slice(
                whole, held[i][k : k + 1], (place_of(col ^ r), 0, i * width)
            )
    mean, square = sums[:total_rows] / D, sums[total_rows:] / D
    inv_std = lax.rsqrt(square - mean * mean + 1e-05)
    normed_rows = ((inputs - mean[:, None]) * inv_std[:, None] * own_vector).astype(BF16)
    cots, norms = [], []
    for c in chunks:
        cots.append(whole[:, c * n : (c + 1) * n].reshape(8 * n, features))
        norms.append(
            jnp.concatenate(
                [
                    lax.dynamic_slice_in_dim(normed_rows, block_at(k) * block_rows + c * n, n, 0)
                    for k in range(8)
                ]
            )
        )

    both, sent = [], []
    for c in chunks:
        left = jnp.where(second, cots[c], norms[c])
        partial = jnp.dot(left, weight, preferred_element_type=F32)
        partial = lax.optimization_barrier(partial)
        both.append(partial[: 4 * n])
        sent.append(exchange(partial[4 * n :].astype(BF16), "row", 1))
    both = [(b + g.astype(F32)).reshape(4, n, hidden) for b, g in zip(both, sent)]
    send = [b[:2].astype(BF16) for b in both]
    later = jnp.where(lax.iota(jnp.int32, features) < 8, 0.0, own_vector)
    high = later.astype(BF16)
    low = (later - high.astype(F32)).astype(BF16)
    gain_rows = jnp.stack([high, low] + [jnp.zeros_like(high)] * 6)
    send[-1], gain_rows, cots, norms = lax.optimization_barrier((send[-1], gain_rows, cots, norms))
    got = [over_y(s, 0) for s in send]
    gain_image = jnp.dot(gain_rows, weight, preferred_element_type=F32)
    gain_image = jnp.sum(gain_image, axis=0, keepdims=True) + image_start
    gain_image = gain_image + exchange(gain_image, "row", 1)
    left = jnp.concatenate([jnp.where(second, cots[c], norms[c]) for c in chunks])
    both = [b[2:] + g.astype(F32) for b, g in zip(both, got)]
    send = [b[:1].astype(BF16) for b in both]
    send[-1], gain_image = lax.optimization_barrier((send[-1], gain_image))
    got = [over_y(s, 1) for s in send]
    gain_image = gain_image + exchange(gain_image, "row", 2)
    mine = [b[1] + g[0].astype(F32) for b, g in zip(both, got)]

    leaving, pullbacks = [], []
    for c in chunks:
        values, pullback = jax.vjp(activation, mine[c])
        leaving.append(jnp.where(second, mine[c], values).astype(BF16))
        pullbacks.append(pullback)
    leaving[-1], gain_image, mean, inv_std = lax.optimization_barrier(
        (leaving[-1], gain_image, mean, inv_std)
    )
    arrived = [exchange(l, "section", 1) for l in leaving]
    gain_image = gain_image + exchange(gain_image, "row", 4)
    first_row = col * block_rows
    own_mean = lax.dynamic_slice_in_dim(mean, first_row, block_rows, 0)
    own_inv = lax.dynamic_slice_in_dim(inv_std, first_row, block_rows, 0)
    own_inputs = lax.dynamic_slice_in_dim(tokens, first_row, block_rows, 0).astype(F32)
    own_centered = (own_inputs - own_mean[:, None]) * own_inv[:, None]
    held = []
    columns = lax.broadcasted_iota(jnp.int32, (n, hidden + 128), 1)
    for c in chunks:
        a, m = arrived[c], mine[c]
        p = jnp.where(second, a, pullbacks[c](a.astype(F32))[0].astype(BF16))
        p, m = lax.optimization_barrier((p, m))
        grads = p.astype(F32)
        a_sum = jnp.sum(grads * gain_image, axis=1, keepdims=True)
        b_sum = jnp.sum(grads * m, axis=1, keepdims=True)
        wide = jnp.pad(p, ((0, 0), (0, 128))).astype(F32)
        wide = jnp.where(columns == hidden, a_sum, wide)
        wide = jnp.where(columns == hidden + 1, b_sum, wide)
        held.append(wide.astype(BF16)[None])
        if c + 1 < CHUNKS:
            arrived[c + 1], _ = lax.optimization_barrier((arrived[c + 1], held[c]))
    got = [over_y(h, 1) for h in held]
    held = [jnp.concatenate([g, h]) for g, h in zip(got, held)]
    held[-1], own_centered, own_inv = lax.optimization_barrier((held[-1], own_centered, own_inv))
    got = [over_y(h, 0) for h in held]
    near = [jnp.concatenate([g, h]).reshape(4 * n, -1) for g, h in zip(got, held)]
    far = [exchange(x, "row", 1) for x in near]

    rights = [jnp.concatenate([x[:, :hidden], f[:, :hidden]]) for x, f in zip(near, far)]
    extras = [jnp.concatenate([x[:, hidden:], f[:, hidden:]]) for x, f in zip(near, far)]
    products = [
        lax.dot_general(r, weight, CONTRACT_LAST, preferred_element_type=F32) for r in rights
    ]
    parts = []
    for p, e in zip(products, extras):
        split = p.reshape(8, n, features)
        beside = e.astype(F32).reshape(8, n, 128)
        blocks = []
        for r in col_order:
            place = place_of(col ^ r)
            blocks.append(
                jnp.concatenate(
                    [
                        lax.dynamic_slice_in_dim(split, place, 1, 0),
                        lax.dynamic_slice_in_dim(beside, place, 1, 0),
                    ],
                    axis=2,
                )
            )
        parts.append(jnp.concatenate(blocks))
    send = [p[:4].astype(BF16) for p in parts]
    products, left = lax.optimization_barrier((products, left))
    gain_grad = jnp.sum(jnp.concatenate(products) * left.astype(F32), axis=0) / own_vector
    bias_grad = jnp.sum(left.astype(F32), axis=0)
    right = jnp.concatenate(rights)
    send[-1], right, gain_grad = lax.optimization_barrier((send[-1], right, gain_grad))
    got = [over_z(s, 0) for s in send]
    gain_grad = gain_grad + exchange(gain_grad, "col", 1)
    right, gain_grad = lax.optimization_barrier((right, gain_grad))
    gain_grad = gain_grad + exchange(gain_grad, "col", 2)
    weight_grads = lax.dot_general(
        left, right, CONTRACT_FIRST, preferred_element_type=F32
    ).astype(BF16)
    weight_grads, got = lax.optimization_barrier((weight_grads, got))
    parts = [p[4:] + g.astype(F32) for p, g in zip(parts, got)]
    send = [p[:2].astype(BF16) for p in parts]
    got = [over_z(x, 1) for x in send]
    gain_grad, _ = lax.optimization_barrier((gain_grad, send))
    other_gain = exchange(gain_grad, "col", 4)
    parts = [p[2:] + g.astype(F32) for p, g in zip(parts, got)]
    got = [exchange(p[0].astype(BF16), "col", 4) for p in parts]
    got[-1], other_gain = lax.optimization_barrier((got[-1], other_gain))
    gain_grad = gain_grad + other_gain
    summed = jnp.concatenate([p[1] + g.astype(F32) for p, g in zip(parts, got)])
    mean_grad = summed[:, features : features + 1] / D
    slope_grad = summed[:, features + 1 : features + 2] / D
    summed = summed[:, :features]
    grad_inputs = own_inv[:, None] * (
        summed * own_vector - mean_grad - own_centered * slope_grad
    )
    output = summed + own_vector
    section_outputs = jnp.where(second, output, grad_inputs).astype(BF16)[None]
    vector_grads = jnp.where(second, bias_grad, gain_grad)[None]
    return (section_outputs, weight_grads[None], vector_grads)


def solution(mesh):
    in_specs = (P(None, "row"), P("section", "row"), P("section", "row", "col"), P("col", "row"))
    out_specs = (P("section", "col", "row"), P("section", "row", "col"), P("section", "row"))
    return jax.shard_map(local, mesh=mesh, in_specs=in_specs, out_specs=out_specs, check_vma=False)
```

```python
import jax
import jax.numpy as jnp
from jax import lax
from jax.sharding import PartitionSpec as P

D = 12288
F32 = jnp.float32
BF16 = jnp.bfloat16
CHUNKS = 2
COL_ORDERS = ((1, 3, 4), (3, 4, 1), (4, 1, 3))
CONTRACT_LAST = (((1,), (1,)), ((), ()))
CONTRACT_FIRST = (((0,), (0,)), ((), ()))


def exchange(block, axis, mask):
    ranks = range(lax.axis_size(axis))
    return lax.ppermute(block, axis, [(i, i ^ mask) for i in ranks])


def mask_of(core, turn):
    return 1 + 2 * (core ^ turn)


def over_y(block, turn):
    ranks = range(lax.axis_size("row"))
    return lax.ppermute(block, "row", [(i, i ^ (2 * mask_of(i % 2, turn))) for i in ranks])


def over_z(block, turn):
    rows, cols = lax.axis_size("row"), lax.axis_size("col")
    route = [
        (r * cols + c, r * cols + (c ^ mask_of(r % 2, turn)))
        for r in range(rows)
        for c in range(cols)
    ]
    return lax.ppermute(block, ("row", "col"), route)


def activation(values):
    return jax.nn.gelu(values, approximate=True)


def local(tokens, vectors, weights, cotangent):
    second = lax.axis_index("section") == 1
    row = lax.axis_index("row")
    col = lax.axis_index("col")
    core = row % 2
    weight = weights[0]
    own_vector = vectors[0]
    features, hidden = weight.shape
    block_rows = cotangent.shape[0]
    n = block_rows // CHUNKS
    total_rows = tokens.shape[0]
    chunks = range(CHUNKS)
    first, then = mask_of(core, 0), mask_of(core, 1)
    col_order = [6, 2, first ^ 4, first, then ^ 4, then, 4, 0]

    def block_at(place):
        other, q = place // 4, place % 4
        y = (2, mask_of(core ^ other, 0), mask_of(core ^ other, 1), 0)[q]
        return row ^ (2 * y + other)

    def place_of(block):
        relative = block ^ row
        y, other = relative // 2, relative % 2
        odd = 1 + ((y // 2) ^ core ^ other)
        return other * 4 + jnp.where(y % 2 == 1, odd, jnp.where(y == 2, 0, 3))

    width = features // 3
    held = [cotangent[None, :, i * width : (i + 1) * width] for i in range(3)]
    relative = [[0], [0], [0]]
    for step in range(3):
        got = [exchange(held[i], "col", order[step]) for i, order in enumerate(COL_ORDERS)]
        if step == 1:
            inputs = tokens.astype(F32)
            sums = jnp.concatenate([jnp.sum(inputs, axis=1), jnp.sum(inputs * inputs, axis=1)])
            sums = sums + exchange(sums, "row", 1)
            image_start = jnp.sum(
                weight[:8].astype(F32) * own_vector[:8, None], axis=0, keepdims=True
            )
        held = [jnp.concatenate([h, g]) for h, g in zip(held, got)]
        relative = [
            rel + [order[step] ^ r for r in rel] for rel, order in zip(relative, COL_ORDERS)
        ]
        if step == 0:
            held, tokens, own_vector = lax.optimization_barrier((held, tokens, own_vector))
        if step == 1:
            held, sums, image_start = lax.optimization_barrier((held, sums, image_start))
    sums = sums + exchange(sums, "row", 2)
    sums = sums + exchange(sums, "row", 4)
    whole = jnp.zeros((8, block_rows, features), BF16)
    for i in range(3):
        for k, r in enumerate(relative[i]):
            whole = lax.dynamic_update_slice(
                whole, held[i][k : k + 1], (place_of(col ^ r), 0, i * width)
            )
    mean, square = sums[:total_rows] / D, sums[total_rows:] / D
    inv_std = lax.rsqrt(square - mean * mean + 1e-05)
    normed_rows = ((inputs - mean[:, None]) * inv_std[:, None] * own_vector).astype(BF16)
    cots, norms = [], []
    for c in chunks:
        cots.append(whole[:, c * n : (c + 1) * n].reshape(8 * n, features))
        norms.append(
            jnp.concatenate(
                [
                    lax.dynamic_slice_in_dim(normed_rows, block_at(k) * block_rows + c * n, n, 0)
                    for k in range(8)
                ]
            )
        )

    both, sent = [], []
    for c in chunks:
        left = jnp.where(second, cots[c], norms[c])
        partial = jnp.dot(left, weight, preferred_element_type=F32)
        partial = lax.optimization_barrier(partial)
        both.append(partial[: 4 * n])
        sent.append(exchange(partial[4 * n :].astype(BF16), "row", 1))
    both = [(b + g.astype(F32)).reshape(4, n, hidden) for b, g in zip(both, sent)]
    send = [b[:2].astype(BF16) for b in both]
    later = jnp.where(lax.iota(jnp.int32, features) < 8, 0.0, own_vector)
    high = later.astype(BF16)
    low = (later - high.astype(F32)).astype(BF16)
    gain_rows = jnp.stack([high, low] + [jnp.zeros_like(high)] * 6)
    gain_rows, cots, norms, _ = lax.optimization_barrier((gain_rows, cots, norms, send))
    got = [over_y(s, 0) for s in send]
    gain_image = jnp.dot(gain_rows, weight, preferred_element_type=F32)
    gain_image = jnp.sum(gain_image, axis=0, keepdims=True) + image_start
    gain_image = gain_image + exchange(gain_image, "row", 1)
    left = jnp.concatenate([jnp.where(second, cots[c], norms[c]) for c in chunks])
    both = [b[2:] + g.astype(F32) for b, g in zip(both, got)]
    send = [b[:1].astype(BF16) for b in both]
    gain_image, _ = lax.optimization_barrier((gain_image, send))
    got = [over_y(s, 1) for s in send]
    gain_image = gain_image + exchange(gain_image, "row", 2)
    mine = [b[1] + g[0].astype(F32) for b, g in zip(both, got)]

    leaving, pullbacks = [], []
    for c in chunks:
        values, pullback = jax.vjp(activation, mine[c])
        leaving.append(jnp.where(second, mine[c], values).astype(BF16))
        pullbacks.append(pullback)
    leaving[-1], gain_image, mean, inv_std = lax.optimization_barrier(
        (leaving[-1], gain_image, mean, inv_std)
    )
    arrived = [exchange(l, "section", 1) for l in leaving]
    gain_image = gain_image + exchange(gain_image, "row", 4)
    first_row = col * block_rows
    own_mean = lax.dynamic_slice_in_dim(mean, first_row, block_rows, 0)
    own_inv = lax.dynamic_slice_in_dim(inv_std, first_row, block_rows, 0)
    own_inputs = lax.dynamic_slice_in_dim(tokens, first_row, block_rows, 0).astype(F32)
    own_centered = (own_inputs - own_mean[:, None]) * own_inv[:, None]
    held = []
    columns = lax.broadcasted_iota(jnp.int32, (n, hidden + 128), 1)
    for c in chunks:
        a, m = arrived[c], mine[c]
        p = jnp.where(second, a, pullbacks[c](a.astype(F32))[0].astype(BF16))
        p, m = lax.optimization_barrier((p, m))
        grads = p.astype(F32)
        a_sum = jnp.sum(grads * gain_image, axis=1, keepdims=True)
        b_sum = jnp.sum(grads * m, axis=1, keepdims=True)
        wide = jnp.pad(p, ((0, 0), (0, 128))).astype(F32)
        wide = jnp.where(columns == hidden, a_sum, wide)
        wide = jnp.where(columns == hidden + 1, b_sum, wide)
        held.append(wide.astype(BF16)[None])
        if c + 1 < CHUNKS:
            arrived[c + 1], _ = lax.optimization_barrier((arrived[c + 1], held[c]))
    got = [over_y(h, 1) for h in held]
    held = [jnp.concatenate([g, h]) for g, h in zip(got, held)]
    held[-1], own_centered, own_inv = lax.optimization_barrier((held[-1], own_centered, own_inv))
    got = [over_y(h, 0) for h in held]
    near = [jnp.concatenate([g, h]).reshape(4 * n, -1) for g, h in zip(got, held)]
    far = [exchange(x, "row", 1) for x in near]

    rights = [jnp.concatenate([x[:, :hidden], f[:, :hidden]]) for x, f in zip(near, far)]
    extras = [jnp.concatenate([x[:, hidden:], f[:, hidden:]]) for x, f in zip(near, far)]
    products = [
        lax.dot_general(r, weight, CONTRACT_LAST, preferred_element_type=F32) for r in rights
    ]
    parts = []
    for p, e in zip(products, extras):
        split = p.reshape(8, n, features)
        beside = e.astype(F32).reshape(8, n, 128)
        blocks = []
        for r in col_order:
            place = place_of(col ^ r)
            blocks.append(
                jnp.concatenate(
                    [
                        lax.dynamic_slice_in_dim(split, place, 1, 0),
                        lax.dynamic_slice_in_dim(beside, place, 1, 0),
                    ],
                    axis=2,
                )
            )
        parts.append(jnp.concatenate(blocks))
    send = [p[:4].astype(BF16) for p in parts]
    products, left = lax.optimization_barrier((products, left))
    gain_grad = jnp.sum(jnp.concatenate(products) * left.astype(F32), axis=0) / own_vector
    bias_grad = jnp.sum(left.astype(F32), axis=0)
    right = jnp.concatenate(rights)
    send[-1], right, gain_grad = lax.optimization_barrier((send[-1], right, gain_grad))
    got = [over_z(s, 0) for s in send]
    gain_grad = gain_grad + exchange(gain_grad, "col", 1)
    right, gain_grad = lax.optimization_barrier((right, gain_grad))
    gain_grad = gain_grad + exchange(gain_grad, "col", 2)
    weight_grads = lax.dot_general(
        left, right, CONTRACT_FIRST, preferred_element_type=F32
    ).astype(BF16)
    weight_grads, got = lax.optimization_barrier((weight_grads, got))
    parts = [p[4:] + g.astype(F32) for p, g in zip(parts, got)]
    send = [p[:2].astype(BF16) for p in parts]
    got = [over_z(x, 1) for x in send]
    gain_grad, _ = lax.optimization_barrier((gain_grad, send))
    other_gain = exchange(gain_grad, "col", 4)
    parts = [p[2:] + g.astype(F32) for p, g in zip(parts, got)]
    got = [exchange(p[0].astype(BF16), "col", 4) for p in parts]
    got[-1], other_gain = lax.optimization_barrier((got[-1], other_gain))
    gain_grad = gain_grad + other_gain
    summed = jnp.concatenate([p[1] + g.astype(F32) for p, g in zip(parts, got)])
    mean_grad = summed[:, features : features + 1] / D
    slope_grad = summed[:, features + 1 : features + 2] / D
    summed = summed[:, :features]
    grad_inputs = own_inv[:, None] * (
        summed * own_vector - mean_grad - own_centered * slope_grad
    )
    output = summed + own_vector
    section_outputs = jnp.where(second, output, grad_inputs).astype(BF16)[None]
    vector_grads = jnp.where(second, bias_grad, gain_grad)[None]
    return (section_outputs, weight_grads[None], vector_grads)


def solution(mesh):
    in_specs = (P(None, "row"), P("section", "row"), P("section", "row", "col"), P("col", "row"))
    out_specs = (P("section", "col", "row"), P("section", "row", "col"), P("section", "row"))
    return jax.shard_map(local, mesh=mesh, in_specs=in_specs, out_specs=out_specs, check_vma=False)
```
